32 devices in a mesh: ctx: 8 (over z, y), head: 4 (over x, core).
Axes of the slice: x: 2, y: 2, z: 4, core: 2. Of those that a mesh axis runs over, the one named last changes fastest.
Arguments:
- conv_input: bfloat16 [6144, 8448], P(('ctx', 'head')), may hold values from -6 to 6
- conv_weight: float32 [4, 8448], replicated, may hold values from -3 to 3
- conv_bias: float32 [8448], replicated, may hold values from -3 to 3
- step_size: float32 [128, 6144], P('head', 'ctx'), may hold values from 0 to 0.12, as said below
- log_decay: float32 [128, 6144], P('head', 'ctx'), may hold values from -0.6 to 0, as said below
- skip_gain: float32 [128], P('head'), may hold values from 0.5 to 2
- grad_output: bfloat16 [6144, 8192], P('ctx', 'head'), may hold values from -6 to 6
Outputs:
- layer_output: bfloat16 [6144, 8192], P('ctx', 'head')
- grad_input: bfloat16 [6144, 8448], P(('ctx', 'head'))
- grad_step: float32 [128, 6144], P('head', 'ctx')
- grad_decay: float32 [128, 6144], P('head', 'ctx')
The draws below stay inside these ranges and needn't reach their ends.
Inputs may be any that keep to these rules, and one draw needn't show every extreme that they name: `step_size`: positive step sizes. `log_decay`: negative logarithms of decays.
All inputs are finite; a program needn't handle non-finite values.
Results may differ from the reference program's by a relative error of at most 0.013.
Values may be sent and summed in bfloat16 or wider, within the bound.
A program may use at most 128 MiB of HBM per device.

```python
import math
from functools import partial
import jax
import jax.numpy as jnp
from jax import lax

HEADS = 128
HEAD_DIM = 64
STATE = 128
CONV_W = 4
BLOCK = 256
INNER = 8192
CONV_CH = 8448
SEQ_DEV = 768
SEQ = 6144
N_HEAD = 4


def rate_fields(key):
    keys = jax.random.split(jax.random.fold_in(key, 7), 8)
    pick = jax.random.uniform(keys[0], (HEADS, 1))
    fast_share = 0.5
    quick_mode = pick < fast_share
    fast_rate = jnp.exp(jax.random.uniform(keys[1], (HEADS, 1), minval=math.log(1.0 / 50.0), maxval=math.log(1.0 / 30.0)))
    slow_rate = jnp.exp(jax.random.uniform(keys[2], (HEADS, 1), minval=math.log(0.05), maxval=math.log(0.5))) / SEQ
    baseline_rate = jnp.where(quick_mode, fast_rate, slow_rate)
    coarse_estimate = jax.random.uniform(keys[3], (HEADS, SEQ), minval=0.5, maxval=1.5)
    split_factor = jnp.exp(jax.random.uniform(keys[4], (HEADS, SEQ // SEQ_DEV), minval=math.log(0.5), maxval=math.log(1.5)))
    split_factor = jnp.repeat(split_factor, SEQ_DEV, axis=1)
    spots = jax.random.randint(keys[5], (2,), 0, SEQ)
    positions = jnp.arange(SEQ)
    match_tally = ((positions == spots[0]) | (positions == spots[1])).astype(jnp.float32)[None, :]
    loss_values = jax.random.uniform(keys[6], (HEADS, 1), minval=0.2, maxval=0.4)
    spike_events = jnp.where(quick_mode, 0.0, jnp.log(1.0 - loss_values)) * match_tally
    decay_factors = -baseline_rate * coarse_estimate * split_factor + spike_events
    steps_drawn = 0.4 * jnp.sqrt(baseline_rate) * jax.random.uniform(keys[7], (HEADS, SEQ), minval=0.5, maxval=1.5)
    return (steps_drawn.astype(jnp.float32), decay_factors.astype(jnp.float32))


def draw_step_size(key, part):
    return rate_fields(key)[0]


def draw_log_decay(key, part):
    return rate_fields(key)[1]


def block_scale(rng, dims, pieces, smallest, top_value):
    level = 1.0
    for dim, parts in pieces:
        steps = jax.random.uniform(jax.random.fold_in(jax.random.fold_in(rng, 6), dim), (parts,), jnp.float32, smallest / len(pieces), top_value / len(pieces))
        level = level * jnp.repeat(jnp.exp(steps), dims[dim] // parts).reshape((-1,) + (1,) * (len(dims) - 1 - dim))
    return level


def centred(key, shape, width, most, shards=(), dtype=jnp.bfloat16):
    level = block_scale(key, shape, shards, -0.22, 0.18) if shards else 1.0
    values = jax.random.normal(key, shape, jnp.float32) * width * level
    return jnp.minimum(jnp.maximum(values, -most), most).astype(dtype)


def setup_inputs(seed: int = 0) -> dict:
    splits = jax.random.split(jax.random.key(seed), 8)
    conv_input = centred(splits[0], (SEQ, CONV_CH), 1.0, 6.0, ((0, 32),))
    conv_weight = centred(splits[1], (CONV_W, CONV_CH), CONV_W ** -0.5, 3.0, (), jnp.float32)
    conv_bias = centred(splits[2], (CONV_CH,), 0.5, 3.0, (), jnp.float32)
    step_size = draw_step_size(jax.random.fold_in(splits[7], 71), 0)
    log_decay = draw_log_decay(jax.random.fold_in(splits[7], 71), 0)
    skip_gain = jnp.clip(0.5 + 1.5 * jax.random.uniform(splits[5], (HEADS,), jnp.float32) ** block_scale(splits[5], (HEADS,), ((0, 4),), -0.2, 0.2), 0.5, 2.0)
    grad_output = centred(splits[6], (SEQ, INNER), 1.0, 6.0, ((0, 8), (1, 4)))
    return dict(conv_input=conv_input, conv_weight=conv_weight, conv_bias=conv_bias, step_size=step_size, log_decay=log_decay, skip_gain=skip_gain, grad_output=grad_output)


def block_increment(features, step_sizes, input_map, log_rates):
    cumulative = jnp.cumsum(log_rates, axis=1)
    to_end = jnp.exp(cumulative[:, -1:] - cumulative) * step_sizes
    weighted = (input_map[None, :, :] * to_end[:, :, None]).astype(jnp.bfloat16)
    increment = jnp.einsum('hsn,shp->hnp', weighted.astype(jnp.float32), features.astype(jnp.float32))
    return (cumulative, increment)

def block_update(skip_gain, carry_state, inputs):
    features, step_sizes, input_map, output_map, log_rates = inputs
    cumulative, increment = block_increment(features, step_sizes, input_map, log_rates)
    length = log_rates.shape[1]
    row_index = lax.broadcasted_iota(jnp.int32, (length, length), 0)
    col_index = lax.broadcasted_iota(jnp.int32, (length, length), 1)
    causal = (row_index >= col_index)[None]
    log_gap = jnp.where(causal, cumulative[:, :, None] - cumulative[:, None, :], 0.0)
    decay_matrix = jnp.where(causal, jnp.exp(log_gap), 0.0)
    affinity = jnp.dot(output_map.astype(jnp.bfloat16), input_map.astype(jnp.bfloat16).T, preferred_element_type=jnp.float32)
    weights = (affinity[None] * decay_matrix * step_sizes[:, None, :]).astype(jnp.bfloat16)
    inside = jnp.einsum('hts,shp->thp', weights.astype(jnp.float32), features.astype(jnp.float32))
    entry_map = (output_map[None, :, :] * jnp.exp(cumulative)[:, :, None]).astype(jnp.bfloat16)
    carried = jnp.einsum('htn,hnp->thp', entry_map.astype(jnp.float32), carry_state.astype(jnp.bfloat16).astype(jnp.float32))
    output = inside + carried + skip_gain[None, :, None] * features.astype(jnp.float32)
    following = jnp.exp(cumulative[:, -1])[:, None, None] * carry_state + increment
    return (following, output)

def sequence_ssd(features, step_sizes, input_map, output_map, log_rates, skip_gain, entering):
    heads_here = step_sizes.shape[0]
    seq_rows = features.shape[0]
    blocks = seq_rows // BLOCK
    head_dim = features.shape[1] // heads_here
    feats_b = features.reshape(blocks, BLOCK, heads_here, head_dim)
    steps_b = step_sizes.reshape(heads_here, blocks, BLOCK).transpose(1, 0, 2)
    input_b = input_map.reshape(blocks, BLOCK, input_map.shape[1])
    output_b = output_map.reshape(blocks, BLOCK, output_map.shape[1])
    rates_b = log_rates.reshape(heads_here, blocks, BLOCK).transpose(1, 0, 2)
    update = jax.checkpoint(partial(block_update, skip_gain))
    leaving, outputs = lax.scan(update, entering, (feats_b, steps_b, input_b, output_b, rates_b))
    return (outputs.reshape(seq_rows, features.shape[1]), leaving)

def conv_forward(conv_input, conv_weight, conv_bias):
    taps_count = conv_weight.shape[0]
    tok_rows = conv_input.shape[0]
    padded = jnp.concatenate([jnp.zeros((taps_count - 1, conv_input.shape[1]), jnp.float32), conv_input.astype(jnp.float32)], axis=0)
    preact = conv_bias[None, :] + conv_weight[0][None, :] * padded[0:tok_rows]
    for offset in range(1, taps_count):
        preact = preact + conv_weight[offset][None, :] * padded[offset:offset + tok_rows]
    return preact

def reference(conv_input, conv_weight, conv_bias, step_size, log_decay, skip_gain, grad_output):
    group_heads = HEADS // N_HEAD

    def forward(inputs_conv, steps_all, rates_all):
        preact = conv_forward(inputs_conv, conv_weight, conv_bias)
        activated = jax.nn.silu(preact).astype(jnp.bfloat16)
        features = activated[:, :INNER].reshape(SEQ, N_HEAD, group_heads * HEAD_DIM).transpose(1, 0, 2)
        input_map = activated[:, INNER:INNER + STATE].astype(jnp.float32)
        output_map = activated[:, INNER + STATE:].astype(jnp.float32)
        input_groups = jnp.broadcast_to(input_map[None], (N_HEAD, SEQ, STATE))
        output_groups = jnp.broadcast_to(output_map[None], (N_HEAD, SEQ, STATE))
        steps_groups = steps_all.reshape(N_HEAD, group_heads, SEQ)
        rates_groups = rates_all.reshape(N_HEAD, group_heads, SEQ)
        skip_groups = skip_gain.reshape(N_HEAD, group_heads)
        entering = jnp.zeros((N_HEAD, group_heads, STATE, HEAD_DIM), jnp.float32)
        outputs, leaving = jax.vmap(sequence_ssd)(features, steps_groups, input_groups, output_groups, rates_groups, skip_groups, entering)
        return outputs.transpose(1, 0, 2).reshape(SEQ, INNER)
    output_full, pullback = jax.vjp(forward, conv_input, step_size, log_decay)
    grad_input, grad_step, grad_decay = pullback(grad_output.astype(jnp.float32))
    return (output_full.astype(jnp.bfloat16), grad_input, grad_step, grad_decay)
```

```python
from functools import partial

import jax
import jax.numpy as jnp
from jax import lax
from jax.experimental import pallas as pl
from jax.experimental.pallas import tpu as pltpu
from jax.sharding import PartitionSpec as P

STATE = 128
BLOCK = 256
GROUP = 8
F32 = jnp.float32
BF16 = jnp.bfloat16
VMEM_LIMIT = 50 * 1024 * 1024


def dot(a, b, ca, cb, precision=None):
    return lax.dot_general(
        a, b, (((ca,), (cb,)), ((), ())), precision=precision, preferred_element_type=F32
    )


def halves(value):
    high = value.astype(BF16)
    return high, (value - high.astype(F32)).astype(BF16)


def head_of_lane(rows, width, head_dim):
    row = lax.broadcasted_iota(jnp.int32, (rows, width), 0)
    lane = lax.broadcasted_iota(jnp.int32, (rows, width), 1)
    return jnp.where(lax.rem(row, GROUP) == lane // head_dim, 1.0, 0.0).astype(BF16)


def expand(rows, width, head_dim):
    high = rows.astype(BF16).astype(F32)
    both = jnp.concatenate([high, rows - high], axis=0).astype(BF16)
    return dot(both, head_of_lane(2 * GROUP, width, head_dim), 0, 0)


def head_sums(value, head_dim):
    pick = head_of_lane(GROUP, value.shape[1], head_dim)
    high, low = halves(value)
    return dot(pick, high, 1, 1) + dot(pick, low, 1, 1)


def earlier_or_same(length):
    row = lax.broadcasted_iota(jnp.int32, (length, length), 0)
    col = lax.broadcasted_iota(jnp.int32, (length, length), 1)
    return jnp.where(row <= col, 1.0, 0.0)


def running_sum(rates):
    return dot(rates, earlier_or_same(rates.shape[1]), 1, 0, lax.Precision.HIGHEST)


def states_kernel(head_dim, x_ref, m_ref, dy_ref, rate_ref, step_ref, inc_ref, gp_ref, dec_ref, pack_ref, t_ref, r_ref, d_ref):
    b = pl.program_id(1)
    width = x_ref.shape[1]
    cum = running_sum(rate_ref[...])
    last = cum[:, BLOCK - 1 :]
    to_end = expand(jnp.exp(last - cum) * step_ref[...], width, head_dim)
    from_start = expand(jnp.exp(cum), width, head_dim)
    xw = (x_ref[...].astype(F32) * to_end).astype(BF16)
    dyw = (dy_ref[...].astype(F32) * from_start).astype(BF16)
    inc = dot(m_ref[:, :STATE], xw, 0, 0)
    gp = dot(m_ref[:, STATE:], dyw, 0, 0)
    dec = from_start[BLOCK - 1 :]
    inc_ref[0] = inc
    gp_ref[0] = gp
    dec_ref[0] = jnp.broadcast_to(dec, (GROUP, width))

    @pl.when(b == 0)
    def _():
        t_ref[...] = inc
        r_ref[...] = gp
        d_ref[...] = jnp.broadcast_to(dec, d_ref.shape)

    @pl.when(b > 0)
    def _():
        t_ref[...] = t_ref[...] * dec + inc
        r_ref[...] = r_ref[...] + d_ref[0:1] * gp
        d_ref[...] = d_ref[...] * dec

    @pl.when(b == pl.num_programs(1) - 1)
    def _():
        decay = d_ref[...]
        high = decay.astype(BF16).astype(F32)
        both = jnp.concatenate([high, decay - high], axis=0).astype(BF16)
        pieces, rows, part = pack_ref.shape
        for i in range(pieces):
            lanes = slice(i * part, (i + 1) * part)
            pack_ref[i, :STATE] = t_ref[:, lanes].astype(BF16)
            pack_ref[i, STATE : 2 * STATE] = r_ref[:, lanes].astype(BF16)
            pack_ref[i, 2 * STATE :] = both[:, lanes]


def chain_kernel(in_ref, out_ref):
    peers, rows, part = in_ref.shape

    def decay(c):
        return in_ref[c, 2 * STATE : 2 * STATE + 1].astype(F32) + in_ref[
            c, 2 * STATE + GROUP : 2 * STATE + GROUP + 1
        ].astype(F32)

    state = jnp.zeros((STATE, part), F32)
    for c in range(peers):
        out_ref[c, :STATE] = state.astype(BF16)
        state = decay(c) * state + in_ref[c, :STATE].astype(F32)
    grad = jnp.zeros((STATE, part), F32)
    for c in range(peers - 1, -1, -1):
        out_ref[c, STATE:] = grad.astype(BF16)
        grad = decay(c) * grad + in_ref[c, STATE : 2 * STATE].astype(F32)


def intra_kernel(head_dim, x_ref, m_ref, dy_ref, rate_ref, step_ref, skip_ref, y_ref, dx_ref, gs_ref, gc_ref, gm_ref, aff_ref, da_ref):
    g = pl.program_id(1)
    width = x_ref.shape[1]
    row = lax.broadcasted_iota(jnp.int32, (BLOCK, BLOCK), 0)
    col = lax.broadcasted_iota(jnp.int32, (BLOCK, BLOCK), 1)
    causal = row >= col

    @pl.when(g == 0)
    def _():
        aff_ref[...] = jnp.where(causal, dot(m_ref[:, STATE:], m_ref[:, :STATE], 1, 1), 0.0)
        da_ref[...] = jnp.zeros_like(da_ref)

    cum = running_sum(rate_ref[...])
    cum_col = cum.T
    x = x_ref[...].astype(F32)
    dy = dy_ref[...]
    steps = expand(step_ref[...], width, head_dim)
    xs = (x * steps).astype(BF16)
    pair = 2 * head_dim
    lane = lax.broadcasted_iota(jnp.int32, (BLOCK, pair), 1)
    ins_parts, back_parts = [], []
    for p in range(GROUP // 2):
        lanes = slice(p * pair, (p + 1) * pair)
        xs_p, dy_p = xs[:, lanes], dy[:, lanes]
        ins, back = 0.0, 0.0
        for k in range(2):
            h = 2 * p + k
            mine = (lane // head_dim) == k
            xs_h = jnp.where(mine, xs_p, jnp.zeros_like(xs_p))
            dy_h = jnp.where(mine, dy_p, jnp.zeros_like(dy_p))
            decay = jnp.exp(jnp.minimum(cum_col[:, h : h + 1] - cum[h : h + 1, :], 0.0))
            weights = (aff_ref[...] * decay).astype(BF16)
            ins = ins + dot(weights, xs_h, 1, 0)
            back = back + dot(weights, dy_h, 0, 0)
            da_ref[...] += dot(dy_h, xs_p, 1, 1) * decay
        ins_parts.append(ins)
        back_parts.append(back)
    ins = jnp.concatenate(ins_parts, axis=1)
    back = jnp.concatenate(back_parts, axis=1)
    skip = skip_ref[0:1]
    dyf = dy.astype(F32)
    y_ref[...] = (ins + skip * x).astype(BF16)
    dx_ref[...] = (steps * back + skip * dyf).astype(BF16)
    gs_ref[...] = head_sums(x * back, head_dim)
    gc_ref[...] = head_sums(dyf * ins, head_dim) - head_sums(xs.astype(F32) * back, head_dim)

    @pl.when(g == pl.num_programs(1) - 1)
    def _():
        da = jnp.where(causal, da_ref[...], 0.0).astype(BF16)
        gm_ref[:, :STATE] = dot(da, m_ref[:, STATE:], 0, 0)
        gm_ref[:, STATE:] = dot(da, m_ref[:, :STATE], 1, 0)


def carry_kernel(head_dim, x_ref, m_ref, dy_ref, rate_ref, step_ref, y1_ref, dx1_ref, gs1_ref, gc1_ref, gm1_ref,
                 inc_ref, gp_ref, dec_ref, enter_ref, y_ref, dx_ref, gs_ref, gd_ref, s_ref, g_ref, dot_ref, acc_ref):
    b, g = pl.program_id(0), pl.program_id(1)
    width = x_ref.shape[1]
    blocks = inc_ref.shape[0]

    @pl.when(b == 0)
    def _():
        pieces = enter_ref.shape[0]
        state = jnp.concatenate([enter_ref[i, :STATE] for i in range(pieces)], axis=1).astype(F32)
        grad = jnp.concatenate([enter_ref[i, STATE:] for i in range(pieces)], axis=1).astype(F32)
        grads = [None] * blocks
        for k in range(blocks - 1, -1, -1):
            grads[k] = grad
            g_ref[k, g] = grad.astype(BF16)
            if k > 0:
                grad = dec_ref[k, 0:1] * grad + gp_ref[k]
        for k in range(blocks):
            s_ref[k, g] = state.astype(BF16)
            state = dec_ref[k, 0:1] * state + inc_ref[k]
            total = jnp.sum(state * grads[k], axis=0, keepdims=True)
            total = jnp.broadcast_to(total, (128, width))
            dot_ref[k, g] = head_sums(total, head_dim)

    cum = running_sum(rate_ref[...])
    ending = jnp.exp(cum[:, BLOCK - 1 :] - cum)
    weight = ending * step_ref[...]
    from_start = expand(jnp.exp(cum), width, head_dim)
    to_end = expand(weight, width, head_dim)
    x = x_ref[...].astype(F32)
    dy = dy_ref[...].astype(F32)
    state, grad = s_ref[b, g], g_ref[b, g]
    in_map, out_map = m_ref[:, :STATE], m_ref[:, STATE:]
    carried = from_start * dot(out_map, state, 1, 0)
    pulled = dot(in_map, grad, 1, 0)
    y_ref[...] = (y1_ref[...].astype(F32) + carried).astype(BF16)
    dx = (dx1_ref[...].astype(F32) + to_end * pulled).astype(BF16)
    lanes = pl.ds(pl.multiple_of(g * width, width), width)
    dx_ref[:, lanes] = dx
    xq = head_sums(x * pulled, head_dim)
    gs_ref[...] = gs1_ref[...] + ending * xq
    gc = gc1_ref[...] + head_sums(dy * carried, head_dim) - weight * xq
    at = lax.broadcasted_iota(jnp.int32, gc.shape, 1)
    gc = gc + jnp.where(at == BLOCK - 1, dot_ref[b, g][:, 0:1], 0.0)
    gd_ref[...] = dot(gc, earlier_or_same(BLOCK), 1, 1, lax.Precision.HIGHEST)
    d_in = dot((x * to_end).astype(BF16), grad, 1, 1)
    d_out = dot((dy * from_start).astype(BF16), state, 1, 1)

    @pl.when(g == 0)
    def _():
        acc_ref[...] = gm1_ref[...]

    acc_ref[:, :STATE] += d_in
    acc_ref[:, STATE:] += d_out

    @pl.when(g == pl.num_programs(1) - 1)
    def _():
        dx_ref[:, dx_ref.shape[1] - 2 * STATE :] = acc_ref[...].astype(BF16)


def params(order):
    return pltpu.CompilerParams(vmem_limit_bytes=VMEM_LIMIT, dimension_semantics=order)


def shifted(value, axis, by):
    peers = lax.axis_size(axis)
    pairs = [(i, i + by) for i in range(peers) if 0 <= i + by < peers]
    return lax.ppermute(value, axis, pairs)


def local(conv_input, conv_weight, conv_bias, step_size, log_decay, skip_gain, grad_output):
    taps_count = conv_weight.shape[0]
    tok_rows, channels = conv_input.shape
    heads_here, seq_rows = step_size.shape
    lanes = grad_output.shape[1]
    head_dim = lanes // heads_here
    peers = lax.axis_size("head")
    ctx = lax.axis_size("ctx")
    blocks = seq_rows // BLOCK
    groups = heads_here // GROUP
    width = GROUP * head_dim
    inner = peers * lanes
    full = lanes + 2 * STATE
    map_at = lanes // (2 * STATE)

    earlier = shifted(conv_input[tok_rows - (taps_count - 1) :], ("ctx", "head"), 1)
    padded = jnp.concatenate([earlier, conv_input], axis=0).astype(F32)
    preact = conv_bias[None, :] + conv_weight[0][None, :] * padded[0:tok_rows]
    for offset in range(1, taps_count):
        preact = preact + conv_weight[offset][None, :] * padded[offset : offset + tok_rows]
    activated, silu_back = jax.vjp(jax.nn.silu, preact)
    activated = activated.astype(BF16)
    maps = activated[:, inner:]
    send = jnp.concatenate(
        [
            jnp.concatenate([activated[:, i * lanes : (i + 1) * lanes], maps], axis=1)
            for i in range(peers)
        ],
        axis=0,
    )
    got = lax.all_to_all(send, "head", split_axis=0, concat_axis=0, tiled=True)

    part = lanes // ctx
    pieces = ctx // groups
    gb = [
        pl.BlockSpec((BLOCK, width), lambda g, b: (b, g)),
        pl.BlockSpec((BLOCK, 2 * STATE), lambda g, b: (b, map_at)),
        pl.BlockSpec((BLOCK, width), lambda g, b: (b, g)),
        pl.BlockSpec((GROUP, BLOCK), lambda g, b: (g, b)),
        pl.BlockSpec((GROUP, BLOCK), lambda g, b: (g, b)),
    ]
    bg = [
        pl.BlockSpec((BLOCK, width), lambda b, g: (b, g)),
        pl.BlockSpec((BLOCK, 2 * STATE), lambda b, g: (b, map_at)),
        pl.BlockSpec((BLOCK, width), lambda b, g: (b, g)),
        pl.BlockSpec((GROUP, BLOCK), lambda b, g: (g, b)),
        pl.BlockSpec((GROUP, BLOCK), lambda b, g: (g, b)),
    ]
    tile = pl.BlockSpec((BLOCK, width), lambda b, g: (b, g))
    rows = pl.BlockSpec((GROUP, BLOCK), lambda b, g: (g, b))
    mapgrad = pl.BlockSpec((BLOCK, 2 * STATE), lambda b, g: (b, 0))

    inc, gp, dec, packed = pl.pallas_call(
        partial(states_kernel, head_dim),
        grid=(groups, blocks),
        in_specs=gb,
        out_specs=[
            pl.BlockSpec((1, STATE, width), lambda g, b: (b, 0, g)),
            pl.BlockSpec((1, STATE, width), lambda g, b: (b, 0, g)),
            pl.BlockSpec((1, GROUP, width), lambda g, b: (b, 0, g)),
            pl.BlockSpec((pieces, 2 * STATE + 2 * GROUP, part), lambda g, b: (g, 0, 0)),
        ],
        out_shape=[
            jax.ShapeDtypeStruct((blocks, STATE, lanes), F32),
            jax.ShapeDtypeStruct((blocks, STATE, lanes), F32),
            jax.ShapeDtypeStruct((blocks, GROUP, lanes), F32),
            jax.ShapeDtypeStruct((ctx, 2 * STATE + 2 * GROUP, part), BF16),
        ],
        scratch_shapes=[
            pltpu.VMEM((STATE, width), F32),
            pltpu.VMEM((STATE, width), F32),
            pltpu.VMEM((GROUP, width), F32),
        ],
        compiler_params=params(("arbitrary", "arbitrary")),
        name="states",
    )(got, got, grad_output, log_decay, step_size)

    mine = lax.all_to_all(packed, "ctx", split_axis=0, concat_axis=0, tiled=True)
    chained = pl.pallas_call(
        chain_kernel,
        out_shape=jax.ShapeDtypeStruct((ctx, 2 * STATE, part), BF16),
        compiler_params=pltpu.CompilerParams(vmem_limit_bytes=VMEM_LIMIT),
        name="chain",
    )(mine)
    entering = lax.all_to_all(chained, "ctx", split_axis=0, concat_axis=0, tiled=True)

    skip = jnp.broadcast_to(jnp.repeat(skip_gain, head_dim)[None, :], (GROUP, lanes))
    y1, dx1, gs1, gc1, gm1 = pl.pallas_call(
        partial(intra_kernel, head_dim),
        grid=(blocks, groups),
        in_specs=bg + [pl.BlockSpec((GROUP, width), lambda b, g: (0, g))],
        out_specs=[tile, tile, rows, rows, mapgrad],
        out_shape=[
            jax.ShapeDtypeStruct((seq_rows, lanes), BF16),
            jax.ShapeDtypeStruct((seq_rows, lanes), BF16),
            jax.ShapeDtypeStruct((heads_here, seq_rows), F32),
            jax.ShapeDtypeStruct((heads_here, seq_rows), F32),
            jax.ShapeDtypeStruct((seq_rows, 2 * STATE), F32),
        ],
        scratch_shapes=[pltpu.VMEM((BLOCK, BLOCK), F32), pltpu.VMEM((BLOCK, BLOCK), F32)],
        compiler_params=params(("arbitrary", "arbitrary")),
        cost_estimate=pl.CostEstimate(
            flops=20_000_000_000, bytes_accessed=20_000_000, transcendentals=6_000_000
        ),
        name="intra",
    )(got, got, grad_output, log_decay, step_size, skip)

    def once(*shape):
        return pl.BlockSpec(shape, lambda b, g: (0, 0, jnp.where(b == 0, g, groups - 1)))

    y, dx, grad_steps, grad_rates = pl.pallas_call(
        partial(carry_kernel, head_dim),
        grid=(blocks, groups),
        in_specs=bg
        + [
            tile,
            tile,
            rows,
            rows,
            mapgrad,
            once(blocks, STATE, width),
            once(blocks, STATE, width),
            once(blocks, GROUP, width),
            pl.BlockSpec((pieces, 2 * STATE, part), lambda b, g: (jnp.where(b == 0, g, groups - 1), 0, 0)),
        ],
        out_specs=[tile, pl.BlockSpec((BLOCK, full), lambda b, g: (b, 0)), rows, rows],
        out_shape=[
            jax.ShapeDtypeStruct((seq_rows, lanes), BF16),
            jax.ShapeDtypeStruct((seq_rows, full), BF16),
            jax.ShapeDtypeStruct((heads_here, seq_rows), F32),
            jax.ShapeDtypeStruct((heads_here, seq_rows), F32),
        ],
        scratch_shapes=[
            pltpu.VMEM((blocks, groups, STATE, width), BF16),
            pltpu.VMEM((blocks, groups, STATE, width), BF16),
            pltpu.VMEM((blocks, groups, GROUP, 128), F32),
            pltpu.VMEM((BLOCK, 2 * STATE), F32),
        ],
        compiler_params=params(("arbitrary", "arbitrary")),
        name="carry",
    )(got, got, grad_output, log_decay, step_size, y1, dx1, gs1, gc1, gm1, inc, gp, dec, entering)

    back = lax.all_to_all(dx, "head", split_axis=0, concat_axis=0, tiled=True)
    back = back.reshape(peers, tok_rows, full)
    map_grads = jnp.sum(back[:, :, lanes:].astype(F32), axis=0).astype(BF16)
    grad_act = jnp.concatenate([back[i, :, :lanes] for i in range(peers)] + [map_grads], axis=1)
    grad_pre = silu_back(grad_act.astype(F32))[0]
    following = shifted(grad_pre[: taps_count - 1], ("ctx", "head"), -1)
    extended = jnp.concatenate([grad_pre, following], axis=0)
    total = conv_weight[taps_count - 1][None, :] * extended[0:tok_rows]
    for offset in range(taps_count - 2, -1, -1):
        begin = taps_count - 1 - offset
        total = total + conv_weight[offset][None, :] * extended[begin : begin + tok_rows]
    return (y, total.astype(BF16), grad_steps, grad_rates)


def solution(mesh):
    return jax.shard_map(
        local,
        mesh=mesh,
        in_specs=(
            P(("ctx", "head"), None),
            P(),
            P(),
            P("head", "ctx"),
            P("head", "ctx"),
            P("head"),
            P("ctx", "head"),
        ),
        out_specs=(P("ctx", "head"), P(("ctx", "head"), None), P("head", "ctx"), P("head", "ctx")),
        check_vma=False,
    )
```

```python
from functools import partial

import jax
import jax.numpy as jnp
from jax import lax
from jax.experimental import pallas as pl
from jax.experimental.pallas import tpu as pltpu
from jax.sharding import PartitionSpec as P

STATE = 128
BLOCK = 256
GROUP = 16
F32 = jnp.float32
BF16 = jnp.bfloat16
VMEM_LIMIT = 50 * 1024 * 1024


def dot(a, b, ca, cb):
    return lax.dot_general(
        a, b, (((ca,), (cb,)), ((), ())), preferred_element_type=F32
    )


def halves(value):
    high = value.astype(BF16)
    return high, (value - high.astype(F32)).astype(BF16)


def head_of_lane(rows, width, head_dim):
    row = lax.broadcasted_iota(jnp.int32, (rows, width), 0)
    lane = lax.broadcasted_iota(jnp.int32, (rows, width), 1)
    return jnp.where(lax.rem(row, GROUP) == lane // head_dim, 1.0, 0.0).astype(BF16)


def expand(rows, width, head_dim):
    high = rows.astype(BF16).astype(F32)
    both = jnp.concatenate([high, rows - high], axis=0).astype(BF16)
    return dot(both, head_of_lane(2 * GROUP, width, head_dim), 0, 0)


def head_sums(value, head_dim):
    pick = head_of_lane(GROUP, value.shape[1], head_dim)
    high, low = halves(value)
    return dot(pick, high, 1, 1) + dot(pick, low, 1, 1)


def earlier_or_same(length):
    row = lax.broadcasted_iota(jnp.int32, (length, length), 0)
    col = lax.broadcasted_iota(jnp.int32, (length, length), 1)
    return jnp.where(row <= col, 1.0, 0.0).astype(BF16)


def triangular(rows, contract):
    high = rows.astype(BF16).astype(F32)
    rest = rows - high
    middle = rest.astype(BF16).astype(F32)
    terms = jnp.concatenate([high, middle, rest - middle, jnp.zeros_like(rows)], axis=0)
    sums = dot(terms.astype(BF16), earlier_or_same(rows.shape[1]), 1, contract)
    return sums[:GROUP] + sums[GROUP : 2 * GROUP] + sums[2 * GROUP : 3 * GROUP]


def running_sum(rates):
    return triangular(rates, 0)


def states_kernel(head_dim, x_ref, m_ref, dy_ref, rate_ref, step_ref, inc_ref, gp_ref, dec_ref, pack_ref, t_ref, r_ref, d_ref):
    b = pl.program_id(1)
    width = x_ref.shape[1]
    cum = running_sum(rate_ref[...])
    last = cum[:, BLOCK - 1 :]
    to_end = expand(jnp.exp(last - cum) * step_ref[...], width, head_dim)
    from_start = expand(jnp.exp(cum), width, head_dim)
    xw = (x_ref[...].astype(F32) * to_end).astype(BF16)
    dyw = (dy_ref[...].astype(F32) * from_start).astype(BF16)
    inc = dot(m_ref[:, :STATE], xw, 0, 0)
    gp = dot(m_ref[:, STATE:], dyw, 0, 0)
    dec = from_start[BLOCK - 1 :]
    inc_ref[0] = inc
    gp_ref[0] = gp
    dec_ref[0] = jnp.broadcast_to(dec, (GROUP, width))

    @pl.when(b == 0)
    def _():
        t_ref[...] = inc
        r_ref[...] = gp
        d_ref[...] = jnp.broadcast_to(dec, d_ref.shape)

    @pl.when(b > 0)
    def _():
        t_ref[...] = t_ref[...] * dec + inc
        r_ref[...] = r_ref[...] + d_ref[0:1] * gp
        d_ref[...] = d_ref[...] * dec

    @pl.when(b == pl.num_programs(1) - 1)
    def _():
        decay = d_ref[...]
        high = decay.astype(BF16).astype(F32)
        both = jnp.concatenate([high, decay - high], axis=0).astype(BF16)
        pieces, rows, part = pack_ref.shape
        for i in range(pieces):
            lanes = slice(i * part, (i + 1) * part)
            pack_ref[i, :STATE] = t_ref[:, lanes].astype(BF16)
            pack_ref[i, STATE : 2 * STATE] = r_ref[:, lanes].astype(BF16)
            pack_ref[i, 2 * STATE :] = both[:, lanes]


def chain_kernel(in_ref, out_ref):
    peers, rows, part = in_ref.shape

    def decay(c):
        return in_ref[c, 2 * STATE : 2 * STATE + 1].astype(F32) + in_ref[
            c, 2 * STATE + GROUP : 2 * STATE + GROUP + 1
        ].astype(F32)

    state = jnp.zeros((STATE, part), F32)
    for c in range(peers):
        out_ref[c, :STATE] = state.astype(BF16)
        state = decay(c) * state + in_ref[c, :STATE].astype(F32)
    grad = jnp.zeros((STATE, part), F32)
    for c in range(peers - 1, -1, -1):
        out_ref[c, STATE:] = grad.astype(BF16)
        grad = decay(c) * grad + in_ref[c, STATE : 2 * STATE].astype(F32)


def intra_kernel(head_dim, x_ref, m_ref, dy_ref, rate_ref, step_ref, skip_ref, *refs):
    y_ref, dx_ref, gs_ref, gc_ref, gm_ref, aff_ref, da_ref = refs[-7:]
    g = pl.program_id(1)
    width = x_ref.shape[1]
    row = lax.broadcasted_iota(jnp.int32, (BLOCK, BLOCK), 0)
    col = lax.broadcasted_iota(jnp.int32, (BLOCK, BLOCK), 1)
    causal = row >= col

    @pl.when(g == 0)
    def _():
        aff_ref[...] = jnp.where(causal, dot(m_ref[:, STATE:], m_ref[:, :STATE], 1, 1), 0.0)
        da_ref[...] = jnp.zeros_like(da_ref)

    cum = running_sum(rate_ref[...])
    cum_col = cum.T
    x = x_ref[...].astype(F32)
    dy = dy_ref[...]
    steps = expand(step_ref[...], width, head_dim)
    xs = (x * steps).astype(BF16)
    pair = 2 * head_dim
    lane = lax.broadcasted_iota(jnp.int32, (BLOCK, pair), 1)
    ins_parts, back_parts = [], []
    for p in range(GROUP // 2):
        lanes = slice(p * pair, (p + 1) * pair)
        xs_p, dy_p = xs[:, lanes], dy[:, lanes]
        ins, back = 0.0, 0.0
        for k in range(2):
            h = 2 * p + k
            mine = (lane // head_dim) == k
            xs_h = jnp.where(mine, xs_p, jnp.zeros_like(xs_p))
            dy_h = jnp.where(mine, dy_p, jnp.zeros_like(dy_p))
            decay = jnp.exp(jnp.minimum(cum_col[:, h : h + 1] - cum[h : h + 1, :], 0.0))
            weights = (aff_ref[...] * decay).astype(BF16)
            ins = ins + dot(weights, xs_h, 1, 0)
            back = back + dot(weights, dy_h, 0, 0)
            da_ref[...] += dot(dy_h, xs_p, 1, 1) * decay
        ins_parts.append(ins)
        back_parts.append(back)
    ins = jnp.concatenate(ins_parts, axis=1)
    back = jnp.concatenate(back_parts, axis=1)
    skip = skip_ref[0:1]
    dyf = dy.astype(F32)
    y_ref[...] = (ins + skip * x).astype(BF16)
    dx_ref[...] = (steps * back + skip * dyf).astype(BF16)
    gs_ref[...] = head_sums(x * back, head_dim)
    gc_ref[...] = head_sums(dyf * ins, head_dim) - head_sums(xs.astype(F32) * back, head_dim)

    @pl.when(g == pl.num_programs(1) - 1)
    def _():
        da = jnp.where(causal, da_ref[...], 0.0).astype(BF16)
        gm_ref[:, :STATE] = dot(da, m_ref[:, STATE:], 0, 0)
        gm_ref[:, STATE:] = dot(da, m_ref[:, :STATE], 1, 0)


def carry_kernel(head_dim, x_ref, m_ref, dy_ref, rate_ref, step_ref, y1_ref, dx1_ref, gs1_ref, gc1_ref, gm1_ref,
                 inc_ref, gp_ref, dec_ref, enter_ref, *refs):
    y_ref, dx_ref, gs_ref, gd_ref, s_ref, g_ref, dot_ref, acc_ref = refs[-8:]
    b, g = pl.program_id(0), pl.program_id(1)
    width = x_ref.shape[1]
    blocks = inc_ref.shape[0]

    @pl.when(b == 0)
    def _():
        pieces = enter_ref.shape[0]
        state = jnp.concatenate([enter_ref[i, :STATE] for i in range(pieces)], axis=1).astype(F32)
        grad = jnp.concatenate([enter_ref[i, STATE:] for i in range(pieces)], axis=1).astype(F32)
        grads = [None] * blocks
        for k in range(blocks - 1, -1, -1):
            grads[k] = grad
            g_ref[k, g] = grad.astype(BF16)
            if k > 0:
                grad = dec_ref[k, 0:1] * grad + gp_ref[k]
        for k in range(blocks):
            s_ref[k, g] = state.astype(BF16)
            state = dec_ref[k, 0:1] * state + inc_ref[k]
            total = jnp.sum(state * grads[k], axis=0, keepdims=True)
            total = jnp.broadcast_to(total, (128, width))
            dot_ref[k, g] = head_sums(total, head_dim)

    cum = running_sum(rate_ref[...])
    ending = jnp.exp(cum[:, BLOCK - 1 :] - cum)
    weight = ending * step_ref[...]
    from_start = expand(jnp.exp(cum), width, head_dim)
    to_end = expand(weight, width, head_dim)
    x = x_ref[...].astype(F32)
    dy = dy_ref[...].astype(F32)
    state, grad = s_ref[b, g], g_ref[b, g]
    in_map, out_map = m_ref[:, :STATE], m_ref[:, STATE:]
    carried = from_start * dot(out_map, state, 1, 0)
    pulled = dot(in_map, grad, 1, 0)
    y_ref[...] = (y1_ref[...].astype(F32) + carried).astype(BF16)
    dx = (dx1_ref[...].astype(F32) + to_end * pulled).astype(BF16)
    lanes = pl.ds(pl.multiple_of(g * width, width), width)
    dx_ref[:, lanes] = dx
    xq = head_sums(x * pulled, head_dim)
    gs_ref[...] = gs1_ref[...] + ending * xq
    gc = gc1_ref[...] + head_sums(dy * carried, head_dim) - weight * xq
    at = lax.broadcasted_iota(jnp.int32, gc.shape, 1)
    gc = gc + jnp.where(at == BLOCK - 1, dot_ref[b, g][:, 0:1], 0.0)
    gd_ref[...] = triangular(gc, 1)
    d_in = dot((x * to_end).astype(BF16), grad, 1, 1)
    d_out = dot((dy * from_start).astype(BF16), state, 1, 1)

    @pl.when(g == 0)
    def _():
        acc_ref[...] = gm1_ref[...]
        for more_ref in refs[:-8]:
            acc_ref[...] += more_ref[...]

    acc_ref[:, :STATE] += d_in
    acc_ref[:, STATE:] += d_out

    @pl.when(g == pl.num_programs(1) - 1)
    def _():
        dx_ref[:, dx_ref.shape[1] - 2 * STATE :] = acc_ref[...].astype(BF16)


def params(order):
    return pltpu.CompilerParams(vmem_limit_bytes=VMEM_LIMIT, dimension_semantics=order)


def shifted(value, axis, by):
    peers = lax.axis_size(axis)
    pairs = [(i, i + by) for i in range(peers) if 0 <= i + by < peers]
    return lax.ppermute(value, axis, pairs)


def local(conv_input, conv_weight, conv_bias, step_size, log_decay, skip_gain, grad_output):
    taps_count = conv_weight.shape[0]
    tok_rows, channels = conv_input.shape
    heads_here, seq_rows = step_size.shape
    lanes = grad_output.shape[1]
    head_dim = lanes // heads_here
    peers = lax.axis_size("head")
    ctx = lax.axis_size("ctx")
    blocks = seq_rows // BLOCK
    groups = heads_here // GROUP
    width = GROUP * head_dim
    inner = peers * lanes
    full = lanes + 2 * STATE
    map_at = lanes // (2 * STATE)

    earlier = shifted(conv_input[tok_rows - (taps_count - 1) :], ("ctx", "head"), 1)
    padded = jnp.concatenate([earlier, conv_input], axis=0).astype(F32)
    preact = conv_bias[None, :] + conv_weight[0][None, :] * padded[0:tok_rows]
    for offset in range(1, taps_count):
        preact = preact + conv_weight[offset][None, :] * padded[offset : offset + tok_rows]
    activated, silu_back = jax.vjp(jax.nn.silu, preact)
    activated = activated.astype(BF16)
    maps = activated[:, inner:]
    send = jnp.concatenate(
        [
            jnp.concatenate([activated[:, i * lanes : (i + 1) * lanes], maps], axis=1)
            for i in range(peers)
        ],
        axis=0,
    )
    got = lax.all_to_all(send, "head", split_axis=0, concat_axis=0, tiled=True)

    part = lanes // ctx
    pieces = ctx // groups
    gb = [
        pl.BlockSpec((BLOCK, width), lambda g, b: (b, g)),
        pl.BlockSpec((BLOCK, 2 * STATE), lambda g, b: (b, map_at)),
        pl.BlockSpec((BLOCK, width), lambda g, b: (b, g)),
        pl.BlockSpec((GROUP, BLOCK), lambda g, b: (g, b)),
        pl.BlockSpec((GROUP, BLOCK), lambda g, b: (g, b)),
    ]
    bg = [
        pl.BlockSpec((BLOCK, width), lambda b, g: (b, g)),
        pl.BlockSpec((BLOCK, 2 * STATE), lambda b, g: (b, map_at)),
        pl.BlockSpec((BLOCK, width), lambda b, g: (b, g)),
        pl.BlockSpec((GROUP, BLOCK), lambda b, g: (g, b)),
        pl.BlockSpec((GROUP, BLOCK), lambda b, g: (g, b)),
    ]
    tile = pl.BlockSpec((BLOCK, width), lambda b, g: (b, g))
    rows = pl.BlockSpec((GROUP, BLOCK), lambda b, g: (g, b))
    mapgrad = pl.BlockSpec((BLOCK, 2 * STATE), lambda b, g: (b, 0))

    inc, gp, dec, packed = pl.pallas_call(
        partial(states_kernel, head_dim),
        grid=(groups, blocks),
        in_specs=gb,
        out_specs=[
            pl.BlockSpec((1, STATE, width), lambda g, b: (b, 0, g)),
            pl.BlockSpec((1, STATE, width), lambda g, b: (b, 0, g)),
            pl.BlockSpec((1, GROUP, width), lambda g, b: (b, 0, g)),
            pl.BlockSpec((pieces, 2 * STATE + 2 * GROUP, part), lambda g, b: (g, 0, 0)),
        ],
        out_shape=[
            jax.ShapeDtypeStruct((blocks, STATE, lanes), F32),
            jax.ShapeDtypeStruct((blocks, STATE, lanes), F32),
            jax.ShapeDtypeStruct((blocks, GROUP, lanes), F32),
            jax.ShapeDtypeStruct((ctx, 2 * STATE + 2 * GROUP, part), BF16),
        ],
        scratch_shapes=[
            pltpu.VMEM((STATE, width), F32),
            pltpu.VMEM((STATE, width), F32),
            pltpu.VMEM((GROUP, width), F32),
        ],
        compiler_params=params(("arbitrary", "arbitrary")),
        name="states",
    )(got, got, grad_output, log_decay, step_size)

    def columns(value):
        return lax.all_to_all(value, "ctx", split_axis=0, concat_axis=0, tiled=True)

    def chain(mine):
        return pl.pallas_call(
            chain_kernel,
            out_shape=jax.ShapeDtypeStruct((ctx, 2 * STATE, part), BF16),
            compiler_params=pltpu.CompilerParams(vmem_limit_bytes=VMEM_LIMIT),
            name="chain",
        )(mine)

    mine = columns(packed)

    skip = jnp.broadcast_to(jnp.repeat(skip_gain, head_dim)[None, :], (GROUP, lanes))
    SHARES = 2 if groups % 2 == 0 else 1
    share = groups // SHARES

    def intra(k, before):
        at = k * share
        wide = pl.BlockSpec((BLOCK, width), lambda b, g: (b, g + at))
        thin = pl.BlockSpec((GROUP, BLOCK), lambda b, g: (g + at, b))
        return pl.pallas_call(
            partial(intra_kernel, head_dim),
            grid=(blocks, share),
            in_specs=[
                wide,
                bg[1],
                wide,
                thin,
                thin,
                pl.BlockSpec((GROUP, width), lambda b, g: (0, g + at)),
            ]
            + [pl.BlockSpec(memory_space=pl.ANY)] * len(before),
            out_specs=[wide, wide, thin, thin, mapgrad],
            out_shape=[
                jax.ShapeDtypeStruct((seq_rows, lanes), BF16),
                jax.ShapeDtypeStruct((seq_rows, lanes), BF16),
                jax.ShapeDtypeStruct((heads_here, seq_rows), F32),
                jax.ShapeDtypeStruct((heads_here, seq_rows), F32),
                jax.ShapeDtypeStruct((seq_rows, 2 * STATE), F32),
            ],
            scratch_shapes=[pltpu.VMEM((BLOCK, BLOCK), F32), pltpu.VMEM((BLOCK, BLOCK), F32)],
            compiler_params=params(("arbitrary", "arbitrary")),
            cost_estimate=pl.CostEstimate(
                flops=10_000_000_000, bytes_accessed=50_000_000, transcendentals=3_000_000
            ),
            input_output_aliases={6 + i: i for i in range(len(before))},
            name="intra",
        )(got, got, grad_output, log_decay, step_size, skip, *before)

    *first, gm1 = intra(0, [])
    mine, first[2] = lax.optimization_barrier((mine, first[2]))
    entering = columns(chain(mine))
    gm2 = []
    if SHARES == 2:
        *first, more = intra(1, first)
        gm2 = [more]

    def once(*shape):
        return pl.BlockSpec(shape, lambda b, g: (0, 0, jnp.where(b == 0, g, groups - 1)))

    y, dx, grad_steps, grad_rates = pl.pallas_call(
        partial(carry_kernel, head_dim),
        grid=(blocks, groups),
        in_specs=bg
        + [
            tile,
            tile,
            rows,
            rows,
            mapgrad,
            once(blocks, STATE, width),
            once(blocks, STATE, width),
            once(blocks, GROUP, width),
            pl.BlockSpec((pieces, 2 * STATE, part), lambda b, g: (jnp.where(b == 0, g, groups - 1), 0, 0)),
        ]
        + [mapgrad] * len(gm2),
        out_specs=[tile, pl.BlockSpec((BLOCK, full), lambda b, g: (b, 0)), rows, rows],
        out_shape=[
            jax.ShapeDtypeStruct((seq_rows, lanes), BF16),
            jax.ShapeDtypeStruct((seq_rows, full), BF16),
            jax.ShapeDtypeStruct((heads_here, seq_rows), F32),
            jax.ShapeDtypeStruct((heads_here, seq_rows), F32),
        ],
        scratch_shapes=[
            pltpu.VMEM((blocks, groups, STATE, width), BF16),
            pltpu.VMEM((blocks, groups, STATE, width), BF16),
            pltpu.VMEM((blocks, groups, GROUP, 128), F32),
            pltpu.VMEM((BLOCK, 2 * STATE), F32),
        ],
        compiler_params=params(("arbitrary", "arbitrary")),
        name="carry",
    )(got, got, grad_output, log_decay, step_size, *first, gm1, inc, gp, dec, entering, *gm2)

    back = lax.all_to_all(dx, "head", split_axis=0, concat_axis=0, tiled=True)
    back = back.reshape(peers, tok_rows, full)
    map_grads = jnp.sum(back[:, :, lanes:].astype(F32), axis=0).astype(BF16)
    grad_act = jnp.concatenate([back[i, :, :lanes] for i in range(peers)] + [map_grads], axis=1)
    grad_pre = silu_back(grad_act.astype(F32))[0]
    following = shifted(grad_pre[: taps_count - 1], ("ctx", "head"), -1)
    extended = jnp.concatenate([grad_pre, following], axis=0)
    total = conv_weight[taps_count - 1][None, :] * extended[0:tok_rows]
    for offset in range(taps_count - 2, -1, -1):
        begin = taps_count - 1 - offset
        total = total + conv_weight[offset][None, :] * extended[begin : begin + tok_rows]
    return (y, total.astype(BF16), grad_steps, grad_rates)


def solution(mesh):
    return jax.shard_map(
        local,
        mesh=mesh,
        in_specs=(
            P(("ctx", "head"), None),
            P(),
            P(),
            P("head", "ctx"),
            P("head", "ctx"),
            P("head"),
            P("ctx", "head"),
        ),
        out_specs=(P("ctx", "head"), P(("ctx", "head"), None), P("head", "ctx"), P("head", "ctx")),
        check_vma=False,
    )
```
